128 devices in a mesh: row: 16 (over z, y), col: 8 (over x, core).
Axes of the slice: x: 4, y: 4, z: 4, core: 2. Of those that a mesh axis runs over, the one named last changes fastest.
Arguments:
- density: float32 [8192, 8192], P('row', 'col'), may hold values from -0.63067231 to 0.63067231, as said below
- pattern_p: int32 [64, 64], replicated, may hold values from 0 to 1, as said below
- pattern_sq: int32 [64, 64], replicated, may hold values from 0 to 1, as said below
- pattern_cube: int32 [64, 64], replicated, may hold values from 0 to 1, as said below
- placement: int32 [64], replicated, may hold values from 0 to 63, each once
Outputs:
- purified: float32 [8192, 8192], P('row', 'col')
The draws below stay inside these ranges and needn't reach their ends.
Inputs may be any that keep to these rules, and one draw needn't show every extreme that they name: density is symmetric. `pattern_p`: symmetric; every diagonal block is kept. `pattern_sq`: symmetric; every diagonal block is kept. `pattern_cube`: symmetric; every diagonal block is kept.
All inputs are finite; a program needn't handle non-finite values.
Results may differ from the reference program's by a relative error of at most 0.000058.
Values sent between devices are 32-bit elements; how exact they have to be, the bound alone decides.
A program may use at most 128 MiB of HBM per device.

```python
import jax
import jax.numpy as jnp
from jax import lax

BLOCK = 128
NB = 64
ORDER = 8192


def mirrored_pattern(key):
    bits = jax.random.randint(key, (NB, NB), 0, 2).astype(jnp.int32)
    rows = jnp.arange(NB, dtype=jnp.int32)[:, None]
    cols = jnp.arange(NB, dtype=jnp.int32)[None, :]
    upper = jnp.where(rows < cols, bits, bits.T)
    return jnp.where(rows == cols, jnp.int32(1), upper).astype(jnp.int32)


def draw_density(key, part):
    key = jax.random.fold_in(key, 11)
    scale = ORDER ** (-0.25)
    first = jax.random.fold_in(key, 0)
    raw = jax.random.normal(first, (ORDER, ORDER), jnp.float32)
    even = (raw + raw.T) * 0.70710678
    return jnp.clip(even * scale, -6.0 * scale, 6.0 * scale).astype(jnp.float32)


def draw_pattern_p(key, part):
    key = jax.random.fold_in(key, 21)
    return mirrored_pattern(key)


def draw_pattern_sq(key, part):
    key = jax.random.fold_in(key, 31)
    return mirrored_pattern(key)


def draw_pattern_cube(key, part):
    key = jax.random.fold_in(key, 41)
    return mirrored_pattern(key)


def setup_inputs(seed: int = 0) -> dict:
    splits = jax.random.split(jax.random.key(seed), 6)
    return {
        "density": draw_density(jax.random.fold_in(splits[5], 71), 0),
        "pattern_p": draw_pattern_p(jax.random.fold_in(splits[5], 71), 0),
        "pattern_sq": draw_pattern_sq(jax.random.fold_in(splits[5], 71), 0),
        "pattern_cube": draw_pattern_cube(jax.random.fold_in(splits[5], 71), 0),
        "placement": jax.random.permutation(splits[4], NB).astype(jnp.int32),
    }


def stored_mask(pattern, placement):
    count = pattern.shape[0]
    onehot = (placement[:, None] == jnp.arange(count, dtype=jnp.int32)[None, :]).astype(jnp.float32)
    moved = jnp.dot(onehot.T, pattern.astype(jnp.float32), precision=lax.Precision.HIGHEST)
    moved = jnp.dot(moved, onehot, precision=lax.Precision.HIGHEST)
    return jnp.repeat(jnp.repeat(moved, BLOCK, axis=0), BLOCK, axis=1)


def reference(density, pattern_p, pattern_sq, pattern_cube, placement):
    kept = density * stored_mask(pattern_p, placement)
    square = jnp.dot(kept, kept, precision=lax.Precision.HIGHEST) * stored_mask(pattern_sq, placement)
    cube = jnp.dot(square, kept, precision=lax.Precision.HIGHEST) * stored_mask(pattern_cube, placement)
    return 3.0 * square - 2.0 * cube
```

```python
import functools

import jax
import jax.numpy as jnp
from jax import lax
from jax.experimental import pallas as pl
from jax.experimental.pallas import tpu as pltpu
from jax.sharding import PartitionSpec as P

BLOCK = 128
MESH = pl.DeviceIdType.MESH
CAPS = (12, 10, 9, 9)
ENDS = (12, 22, 31, 40)
STARTS = (0, 12, 22, 31)
SLOTS = 40
ZERO = tuple(8 * cap for cap in CAPS)
FIRST = 16


def local_mask(stored, row_start, col_start, row_blocks, col_blocks):
    piece = lax.dynamic_slice(stored, (row_start, col_start), (row_blocks, col_blocks))
    return jnp.repeat(jnp.repeat(piece, BLOCK, axis=0), BLOCK, axis=1)


def dense(density, stored_p, stored_sq, stored_cube):
    row_blocks = density.shape[0] // BLOCK
    col_blocks = density.shape[1] // BLOCK
    row_start = lax.axis_index("row") * row_blocks
    col_start = lax.axis_index("col") * col_blocks
    kept = density * local_mask(stored_p, row_start, col_start, row_blocks, col_blocks)
    mask_sq = local_mask(stored_sq, row_start, col_start, row_blocks, col_blocks)
    mask_cube = local_mask(stored_cube, row_start, col_start, row_blocks, col_blocks)
    kept_panel = lax.all_gather(kept, "col", axis=1, tiled=True)
    columns = lax.all_gather(kept, "row", axis=0, tiled=True)
    square = jnp.dot(kept_panel, columns, precision=lax.Precision.HIGHEST) * mask_sq
    square_panel = lax.all_gather(square, "col", axis=1, tiled=True)
    cube = jnp.dot(square_panel, columns, precision=lax.Precision.HIGHEST) * mask_cube
    return 3.0 * square - 2.0 * cube


def before(x, through=False):
    size = x.shape[-1]
    tri = jnp.arange(size)[:, None] < jnp.arange(size)[None, :] + int(through)
    sums = jnp.dot(x.astype(jnp.float32), tri.astype(jnp.float32), precision=lax.Precision.HIGHEST)
    return sums.astype(jnp.int32)


def plan(stored_p, row, col):
    z, y = row // 4, row % 4
    kept = stored_p.astype(jnp.int32)
    x = kept.reshape(4, 4, 4, 8, 4, 2).transpose(3, 0, 1, 4, 2, 5).reshape(8, 4, 4, 4, 8)
    n = x.sum(-1)
    total = before(n, True).astype(jnp.float32)
    whole = total.sum((1, 2), keepdims=True)
    by_z = total.sum(2, keepdims=True)
    by_y = total.sum(1, keepdims=True)
    even = (jnp.arange(4)[:, None] + jnp.arange(4)[None, :]) % 2
    dither = (even.astype(jnp.float32) * 0.5 + 0.25)[None, :, :, None]
    target = jnp.floor(total / 2 + (by_y - by_z) / 8 + dither).astype(jnp.int32)
    have = jnp.zeros(n.shape[:3], jnp.int32)
    incs = []
    for q in range(4):
        inc = jnp.clip(target[..., q] - have, 0, n[..., q])
        have = have + inc
        incs.append(inc)
    inc = jnp.stack(incs, -1)
    first = x * (before(x) < inc[..., None]).astype(jnp.int32)
    second = x - first
    ok = jnp.bool_(True)
    for s in (first, second):
        ok = ok & jnp.all(s.sum((3, 4)) <= FIRST)

    def ordered(s, members):
        g = s.transpose(0, 1, 3, 2, 4) if members == "y" else s.transpose(0, 2, 3, 1, 4)
        flat = g.reshape(8, 4, 4, 32)
        cnt = flat.sum(-1)
        start = jnp.zeros((8, 4), jnp.int32)
        good = jnp.bool_(True)
        starts = []
        for q in range(4):
            start = jnp.maximum(start, STARTS[max(q - 1, 0)])
            starts.append(start)
            start = start + cnt[..., q]
            good = good & jnp.all(start <= ENDS[q])
        pos = jnp.stack(starts, -1)[..., None] + before(flat)
        pos = pos.reshape(8, 4, 4, 4, 8)
        pos = pos.transpose(0, 1, 3, 2, 4) if members == "y" else pos.transpose(0, 3, 1, 2, 4)
        return pos, good

    pos0, good0 = ordered(first, "y")
    pos1, good1 = ordered(second, "z")
    ok = ok & good0 & good1

    take = lambda t: lax.dynamic_index_in_dim(t, col, 0, keepdims=False)
    first, second, pos0, pos1 = (take(t) for t in (first, second, pos0, pos1))
    at0 = before(first.reshape(4, 4, 32)).reshape(4, 4, 4, 8)
    at1 = before(second.reshape(4, 4, 32)).reshape(4, 4, 4, 8)

    ids = (
        jnp.arange(4)[:, None, None] * 2
        + jnp.arange(4)[None, :, None] * 8
        + jnp.arange(2)[None, None, :]
    ).reshape(32)
    slots = jnp.arange(FIRST)
    own = lambda t: t[z, y].reshape(32)
    pack = [
        jnp.sum(jnp.where((own(a)[None] == slots[:, None]) & (own(s)[None] > 0), ids[None], 0), -1)
        for s, a in ((first, at0), (second, at1))
    ]
    member = jnp.arange(4)[:, None, None] * FIRST
    places = jnp.arange(SLOTS)
    gather = []
    for s, a, p in (
        (first[z], at0[z], pos0[z]),
        (second[:, y], at1[:, y], pos1[:, y]),
    ):
        src = (member + a).reshape(128)
        hit = (p.reshape(128)[None] == places[:, None]) & (s.reshape(128)[None] > 0)
        gather.append(jnp.sum(jnp.where(hit, src[None], 0), -1))
    group0 = jnp.arange(4)[:, None, None, None]
    group1 = 4 + jnp.arange(4)[None, :, None, None]
    locs = []
    for q in range(4):
        f, s = first[:, :, q], second[:, :, q]
        pos = jnp.where(f > 0, pos0[:, :, q], pos1[:, :, q])
        group = jnp.where(f > 0, group0[:, :, 0], group1[:, :, 0])
        there = (f + s) > 0
        late = pos >= STARTS[q]
        cur = jnp.where(there & late, group * CAPS[q] + pos - STARTS[q], ZERO[q])
        p = max(q - 1, 0)
        prev = jnp.where(there & ~late, group * CAPS[p] + pos - STARTS[p], ZERO[p])
        locs.append(jnp.stack([prev, cur], -1).reshape(256))
    return ok, jnp.concatenate(pack), jnp.concatenate(gather), jnp.concatenate(locs)


def split(x):
    hi = x.astype(jnp.bfloat16)
    lo = (x - hi.astype(jnp.float32)).astype(jnp.bfloat16)
    return hi, lo


def product(left, right):
    lh, ll = split(left)
    rh, rl = split(right)
    lhs = jnp.concatenate([lh, lh, ll], axis=1)
    rhs = jnp.concatenate([rh, rl, rh], axis=0)
    return jnp.dot(lhs, rhs, preferred_element_type=jnp.float32)


class Ring:
    def __init__(self, part, size, me, plus, minus, ss, rs, base):
        up, down = lax.rem(me + 1, 4), lax.rem(me + 3, 4)
        cut = (size + 1) // 2
        own, left, right = part(me, 0, size), part(down, 0, size), part(up, 0, size)
        copy = lambda ref, n, dev: pltpu.make_async_remote_copy(
            src_ref=ref,
            dst_ref=ref,
            send_sem=ss.at[base + n],
            recv_sem=rs.at[base + n],
            device_id=dev,
            device_id_type=MESH,
        )
        self.copies = [
            copy(own, 0, plus),
            copy(own, 1, minus),
            copy(part(down, 0, cut), 2, plus),
            copy(part(up, cut, size - cut), 3, minus),
        ]

    def near(self):
        self.copies[0].start()
        self.copies[1].start()

    def far(self):
        self.copies[0].wait_recv()
        self.copies[2].start()
        self.copies[1].wait_recv()
        self.copies[3].start()

    def done(self):
        self.copies[2].wait_recv()
        self.copies[3].wait_recv()

    def sent(self):
        for c in self.copies:
            c.wait_send()


class Twin:
    def __init__(self, part, size, me, twin, ss, rs, base):
        self.copies = []
        for n in range(4):
            ref = part(lax.rem(me + n, 4), 0, size)
            self.copies.append(
                pltpu.make_async_remote_copy(
                    src_ref=ref,
                    dst_ref=ref,
                    send_sem=ss.at[base + n],
                    recv_sem=rs.at[base + n],
                    device_id=twin,
                    device_id_type=MESH,
                )
            )

    def start(self, *which):
        for n in which:
            self.copies[n].start()

    def recv(self, *which):
        for n in which:
            self.copies[n].wait_recv()

    def sent(self):
        for c in self.copies:
            c.wait_send()


COPIES = 8 + 8 + 4 * 8 + 4 * 8


def kernel(
    dens, pack, gather, locs, mask_p, mask_sq, mask_cube,
    out,
    a_buf, g0, g1, b0, b1, b2, b3, s2, s3, acc, ss, rs, own_sem,
):
    row, col = lax.axis_index("row"), lax.axis_index("col")
    z, y, x, core = row // 4, lax.rem(row, 4), col // 2, lax.rem(col, 2)
    up = lambda v: lax.rem(v + 1, 4)
    down = lambda v: lax.rem(v + 3, 4)
    yp, ym = (z * 4 + up(y), col), (z * 4 + down(y), col)
    zp, zm = (up(z) * 4 + y, col), (down(z) * 4 + y, col)
    xp, xm = (row, up(x) * 2 + core), (row, down(x) * 2 + core)
    twin = (row, x * 2 + 1 - core)
    pieces = (b0, b1, b2, b3)
    squares = (g0, g1, s2, s3)

    barrier = pltpu.get_barrier_semaphore()
    for dev in (yp, ym, zp, zm, xp, xm, twin):
        pl.semaphore_signal(barrier, inc=1, device_id=dev, device_id_type=MESH)

    mine = pltpu.make_async_copy(dens, a_buf.at[col], own_sem)
    mine.start()
    zero = jnp.zeros((BLOCK, BLOCK), jnp.float32)
    for piece, at in zip(pieces, ZERO):
        piece[at] = zero

    for i in range(4):
        for j in range(8):
            s2[i * 8 + j] = dens[i * BLOCK : (i + 1) * BLOCK, j * BLOCK : (j + 1) * BLOCK]

    def fill(s, _):
        g0[y * FIRST + s] = s2[pack[s]]
        g1[z * FIRST + s] = s2[pack[FIRST + s]]
        return 0

    lax.fori_loop(0, FIRST, fill, 0)
    mine.wait()

    base = 0
    a_part = lambda m, lo, n: a_buf.at[m * 2 + core, pl.ds(lo, n)]
    a_ring = Ring(a_part, 512, x, xp, xm, ss, rs, base)
    a_twin = Twin(a_part, 512, x, twin, ss, rs, base + 4)
    base += 8
    g_rings = [
        Ring(lambda m, lo, n: g0.at[pl.ds(m * FIRST + lo, n)], FIRST, y, yp, ym, ss, rs, base),
        Ring(lambda m, lo, n: g1.at[pl.ds(m * FIRST + lo, n)], FIRST, z, zp, zm, ss, rs, base + 4),
    ]
    base += 8
    b_rings = []
    for piece, cap in zip(pieces, CAPS):
        part0 = lambda m, lo, n, r=piece, c=cap: r.at[pl.ds(m * c + lo, n)]
        part1 = lambda m, lo, n, r=piece, c=cap: r.at[pl.ds((4 + m) * c + lo, n)]
        b_rings.append([
            Ring(part0, cap, z, zp, zm, ss, rs, base),
            Ring(part1, cap, y, yp, ym, ss, rs, base + 4),
        ])
        base += 8
    s_rings, s_twins = [], []
    for sq in squares:
        part = lambda m, lo, n, r=sq: r.at[pl.ds((m * 2 + core) * 8 + lo, n)]
        s_rings.append(Ring(part, 8, x, xp, xm, ss, rs, base))
        s_twins.append(Twin(part, 8, x, twin, ss, rs, base + 4))
        base += 8

    near = lambda rings: [r.near() for r in rings]
    far = lambda rings: [r.far() for r in rings]
    done = lambda rings: [r.done() for r in rings]

    pl.semaphore_wait(barrier, 7)
    near(g_rings)
    a_ring.near()
    a_twin.start(0)
    far(g_rings)
    done(g_rings)

    for q in range(4):

        def regroup(s, _, q=q):
            pieces[q][z * CAPS[q] + s] = g0[gather[STARTS[q] + s]]
            pieces[q][(4 + y) * CAPS[q] + s] = g1[gather[SLOTS + STARTS[q] + s]]
            return 0

        lax.fori_loop(0, CAPS[q], regroup, 0)
        if q < 2:
            near(b_rings[q])
    for r in g_rings:
        r.sent()

    def right_block(q, k, jj):
        at = ((q * 64 + k) * 2 + jj) * 2
        block = pieces[q][locs[at + 1]]
        if q:
            block = block + pieces[q - 1][locs[at]]
        return block

    def square(q):
        acc[...] = jnp.zeros_like(acc)

        def step(kk, _):
            k0 = kk * 4
            a = a_buf[kk // 2, :, pl.ds(pl.multiple_of(lax.rem(kk, 2) * 512, 512), 512)]
            left = jnp.concatenate([
                jnp.concatenate([
                    a[i * BLOCK : (i + 1) * BLOCK, t * BLOCK : (t + 1) * BLOCK] * mask_p[i * 64 + k0 + t]
                    for t in range(4)
                ], axis=1)
                for i in range(4)
            ], axis=0)
            right = jnp.concatenate([
                jnp.concatenate([right_block(q, k0 + t, jj) for jj in range(2)], axis=1)
                for t in range(4)
            ], axis=0)
            acc[...] += product(left, right)
            return 0

        lax.fori_loop(0, 16, step, 0)
        for i in range(4):
            for jj in range(2):
                squares[q][col * 8 + i * 2 + jj] = (
                    acc[i * BLOCK : (i + 1) * BLOCK, jj * BLOCK : (jj + 1) * BLOCK]
                    * mask_sq[i * 8 + 2 * q + jj]
                )
        s_rings[q].near()
        s_twins[q].start(0)

    def cube(q):
        def step(cd, _):
            left = jnp.concatenate([
                jnp.concatenate([squares[q][cd * 8 + i * 2 + t] for t in range(2)], axis=1)
                for i in range(4)
            ], axis=0)
            for n in range(4):
                right = jnp.concatenate([
                    jnp.concatenate([right_block(n, cd * 8 + 2 * q + t, jj) for jj in range(2)], axis=1)
                    for t in range(2)
                ], axis=0)
                out[:, n * 256 : (n + 1) * 256] += product(left, right)
            return 0

        lax.fori_loop(0, 8, step, 0)

    far(b_rings[0])
    near(b_rings[2])
    a_ring.far()
    a_twin.start(1, 3)
    done(b_rings[0])
    far(b_rings[1])
    near(b_rings[3])
    a_ring.done()
    a_twin.start(2)
    a_twin.recv(0, 1, 2, 3)
    square(0)
    done(b_rings[1])
    far(b_rings[2])
    square(1)
    s_rings[0].far()
    s_twins[0].start(1, 3)
    done(b_rings[2])
    far(b_rings[3])
    square(2)
    s_rings[0].done()
    s_twins[0].start(2)
    s_rings[1].far()
    s_twins[1].start(1, 3)
    out[...] = jnp.zeros_like(out)
    done(b_rings[3])
    square(3)
    s_rings[1].done()
    s_twins[1].start(2)
    s_rings[2].far()
    s_twins[2].start(1, 3)
    s_twins[0].recv(0, 1, 2, 3)
    cube(0)
    s_rings[2].done()
    s_twins[2].start(2)
    s_rings[3].far()
    s_twins[3].start(1, 3)
    s_twins[1].recv(0, 1, 2, 3)
    cube(1)
    s_rings[3].done()
    s_twins[3].start(2)
    s_twins[2].recv(0, 1, 2, 3)
    cube(2)
    s_twins[3].recv(0, 1, 2, 3)
    cube(3)
    for i in range(4):
        for q in range(4):
            for jj in range(2):
                j = 2 * q + jj
                at = (slice(i * BLOCK, (i + 1) * BLOCK), slice(j * BLOCK, (j + 1) * BLOCK))
                out[at] = 3.0 * squares[q][col * 8 + i * 2 + jj] - 2.0 * (out[at] * mask_cube[i * 8 + j])

    a_ring.sent()
    a_twin.sent()
    for pair in b_rings:
        for r in pair:
            r.sent()
    for r in s_rings + s_twins:
        r.sent()


def packed(density, pack, gather, locs, mask_p, mask_sq, mask_cube):
    smem = pl.BlockSpec(memory_space=pltpu.SMEM)
    vmem = pl.BlockSpec(memory_space=pltpu.VMEM)
    blocks = lambda n: pltpu.VMEM((n, BLOCK, BLOCK), jnp.float32)
    return pl.pallas_call(
        kernel,
        out_shape=jax.ShapeDtypeStruct(density.shape, jnp.float32),
        in_specs=[vmem] + [smem] * 6,
        out_specs=vmem,
        scratch_shapes=[
            pltpu.VMEM((8, 512, 1024), jnp.float32),
            blocks(64),
            blocks(64),
            *[blocks(at + 1) for at in ZERO],
            blocks(64),
            blocks(64),
            pltpu.VMEM((512, 256), jnp.float32),
            pltpu.SemaphoreType.DMA((COPIES,)),
            pltpu.SemaphoreType.DMA((COPIES,)),
            pltpu.SemaphoreType.DMA,
        ],
        compiler_params=pltpu.CompilerParams(
            collective_id=0, has_side_effects=True, vmem_limit_bytes=62 * 2**20
        ),
        cost_estimate=pl.CostEstimate(flops=6 * 2**34, bytes_accessed=2**22, transcendentals=0),
    )(density, pack, gather, locs, mask_p, mask_sq, mask_cube)


def body(density, pattern_p, pattern_sq, pattern_cube, placement):
    count = pattern_p.shape[0]
    row, col = lax.axis_index("row"), lax.axis_index("col")
    onehot = (placement[:, None] == jnp.arange(count, dtype=jnp.int32)[None, :]).astype(jnp.float32)

    def stored(pattern):
        moved = jnp.dot(onehot.T, pattern.astype(jnp.float32), precision=lax.Precision.HIGHEST)
        return jnp.dot(moved, onehot, precision=lax.Precision.HIGHEST)

    sp, ssq, scb = stored(pattern_p), stored(pattern_sq), stored(pattern_cube)
    ok, pack, gather, locs = plan(sp, row, col)
    mask_p = lax.dynamic_slice(sp, (row * 4, 0), (4, 64)).reshape(256)
    mask_sq = lax.dynamic_slice(ssq, (row * 4, col * 8), (4, 8)).reshape(32)
    mask_cube = lax.dynamic_slice(scb, (row * 4, col * 8), (4, 8)).reshape(32)
    return lax.cond(
        ok,
        lambda: packed(density, pack, gather, locs, mask_p, mask_sq, mask_cube),
        lambda: dense(density, sp, ssq, scb),
    )


def solution(mesh):
    return jax.shard_map(
        body,
        mesh=mesh,
        in_specs=(P("row", "col"), P(), P(), P(), P()),
        out_specs=P("row", "col"),
        check_vma=False,
    )
```

```python
import functools

import jax
import jax.numpy as jnp
from jax import lax
from jax.experimental import pallas as pl
from jax.experimental.pallas import tpu as pltpu
from jax.sharding import PartitionSpec as P

BLOCK = 128
MESH = pl.DeviceIdType.MESH
CAPS = (12, 10, 9, 9)
ENDS = (12, 22, 31, 40)
STARTS = (0, 12, 22, 31)
SLOTS = 40
ZERO = tuple(8 * cap for cap in CAPS)
FIRST = 16


def local_mask(stored, row_start, col_start, row_blocks, col_blocks):
    piece = lax.dynamic_slice(stored, (row_start, col_start), (row_blocks, col_blocks))
    return jnp.repeat(jnp.repeat(piece, BLOCK, axis=0), BLOCK, axis=1)


def dense(density, pattern_p, pattern_sq, pattern_cube, placement):
    count = pattern_p.shape[0]
    row_blocks = density.shape[0] // BLOCK
    col_blocks = density.shape[1] // BLOCK
    row_start = lax.axis_index("row") * row_blocks
    col_start = lax.axis_index("col") * col_blocks
    onehot = (placement[:, None] == jnp.arange(count, dtype=jnp.int32)[None, :]).astype(jnp.float32)

    def stored(pattern):
        moved = jnp.dot(onehot.T, pattern.astype(jnp.float32), precision=lax.Precision.HIGHEST)
        return jnp.dot(moved, onehot, precision=lax.Precision.HIGHEST)

    stored_p, stored_sq, stored_cube = (stored(p) for p in (pattern_p, pattern_sq, pattern_cube))
    kept = density * local_mask(stored_p, row_start, col_start, row_blocks, col_blocks)
    mask_sq = local_mask(stored_sq, row_start, col_start, row_blocks, col_blocks)
    mask_cube = local_mask(stored_cube, row_start, col_start, row_blocks, col_blocks)
    kept_panel = lax.all_gather(kept, "col", axis=1, tiled=True)
    columns = lax.all_gather(kept, "row", axis=0, tiled=True)
    square = jnp.dot(kept_panel, columns, precision=lax.Precision.HIGHEST) * mask_sq
    square_panel = lax.all_gather(square, "col", axis=1, tiled=True)
    cube = jnp.dot(square_panel, columns, precision=lax.Precision.HIGHEST) * mask_cube
    return 3.0 * square - 2.0 * cube


LOC, LISTS, ROWS = 0, 64, 72


def place():
    return lax.axis_index("row"), lax.axis_index("col")


def plan_kernel(where, pat_p, pat_sq, pat_cube, placement, ints, floats, fits):
    row, col = where()
    z, y = row // 4, lax.rem(row, 4)
    f32, bf16 = jnp.float32, jnp.bfloat16

    def grid(shape):
        return lax.broadcasted_iota(jnp.int32, shape, 0), lax.broadcasted_iota(jnp.int32, shape, 1)

    def mm(*terms):
        out = terms[0]
        for t in terms[1:]:
            out = jnp.dot(out.astype(bf16), t.astype(bf16), preferred_element_type=f32)
        return out

    def one(cond):
        return jnp.where(cond, 1.0, 0.0).astype(f32)

    a, b = grid((64, 64))
    onehot_t = one(placement[...] == a)

    def stored(pattern):
        moved = mm(onehot_t, pattern[...].astype(f32))
        return lax.dot_general(
            moved.astype(bf16), onehot_t.astype(bf16), (((1,), (1,)), ((), ())), preferred_element_type=f32
        )

    sp, ssq, scb = stored(pat_p), stored(pat_sq), stored(pat_cube)

    d, k = grid((16, 64))
    device_rows = one(k // 4 == d)
    k2, d2 = grid((64, 16))
    rows_device = one(k2 // 4 == d2)
    j, c = grid((64, 8))
    c2, j2 = grid((8, 64))
    pair = [one((j // 8 == c) & (lax.rem(j, 8) // 2 == q)) for q in range(4)]
    pair_t = [one((j2 // 8 == c2) & (lax.rem(j2, 8) // 2 == q)) for q in range(4)]
    same_pair = one(a // 2 == b // 2)
    pair_before = one((a // 2 == b // 2) & (a < b))
    pairs_before = one((a // 8 == b // 8) & (a // 2 < b // 2))
    device = a // 4 == b // 4
    rows_before = one(device & (b < a))
    rows_device_all = one(device)
    d3, d4 = grid((16, 16))
    mean = (one(lax.rem(d3, 4) == lax.rem(d4, 4)) - one(d3 // 4 == d4 // 4)) * 0.125
    dd, _ = grid((16, 8))
    dither = (lax.rem(dd // 4 + lax.rem(dd, 4), 2)).astype(f32) * 0.5 + 0.25

    by_device = mm(device_rows, sp)
    total = jnp.zeros((16, 8), f32)
    have = jnp.zeros((16, 8), f32)
    share = jnp.zeros((64, 64), f32)
    for q in range(4):
        n = mm(by_device, pair[q])
        total = total + n
        target = jnp.floor(total * 0.5 + mm(mean, total) + dither)
        inc = jnp.minimum(jnp.maximum(target - have, 0.0), n)
        have = have + inc
        share = share + mm(mm(rows_device, inc), pair_t[q])
    rest = total - have
    worst = jnp.maximum(jnp.max(have - FIRST), jnp.max(rest - FIRST))

    rank = mm(mm(rows_before, sp), same_pair) + mm(sp, pair_before)
    first = sp * one(rank < share)
    second = sp - first

    routes = []
    for sel, group_of in ((first, lambda r: r // 16), (second, lambda r: lax.rem(r // 4, 4))):
        g, kk = grid((8, 64))
        group_rows = one(group_of(kk) == g)
        kk2, g2 = grid((64, 8))
        rows_group = one(group_of(kk2) == g2)
        by_group = mm(group_rows, sel)
        start = jnp.zeros((8, 8), f32)
        base = jnp.zeros((64, 64), f32)
        for q in range(4):
            start = jnp.maximum(start, float(STARTS[max(q - 1, 0)]))
            base = base + mm(mm(rows_group, start), pair_t[q])
            start = start + mm(by_group, pair[q])
            worst = jnp.maximum(worst, jnp.max(start - ENDS[q]))
        order = one((group_of(a) == group_of(b)) & (b < a))
        in_pair = mm(sel, pair_before)
        pos = base + mm(mm(order, sel), same_pair) + in_pair
        slot = mm(mm(rows_device_all, sel), pairs_before) + mm(mm(rows_before, sel), same_pair) + in_pair
        routes.append((pos, slot))
    fits[0, 0] = jnp.where(worst <= 0.0, 1, 0)

    mine = one((j // 8 == col) & (lax.rem(j, 8) == c))
    panel = lambda t: mm(t, mine).astype(jnp.int32)
    sel0, sel1 = panel(first), panel(second)
    pos0, pos1 = panel(routes[0][0]), panel(routes[1][0])
    slot0, slot1 = panel(routes[0][1]), panel(routes[1][1])
    r, jl = grid((64, 8))
    pos = jnp.where(sel0 > 0, pos0, pos1)
    group = jnp.where(sel0 > 0, r // 16, 4 + lax.rem(r // 4, 4))
    there = (sel0 + sel1) > 0
    q = jl // 2
    table = lambda values: sum(jnp.where(q == n, v, 0) for n, v in enumerate(values))
    early = tuple(max(n - 1, 0) for n in range(4))
    late = pos >= table(STARTS)
    cur = jnp.where(there & late, group * table(CAPS) + pos - table(STARTS), table(ZERO))
    prev_caps = table([CAPS[p] for p in early])
    prev_start = table([STARTS[p] for p in early])
    prev_zero = table([ZERO[p] for p in early])
    prev = jnp.where(there & ~late, group * prev_caps + pos - prev_start, prev_zero)
    ints[LOC : LOC + 64, 0:8] = prev
    ints[LOC : LOC + 64, 8:16] = cur

    rr, lane = grid((64, 128))
    ids = lax.rem(rr, 4) * 8
    lists = [jnp.zeros((64, 128), jnp.int32) for _ in range(4)]
    for n in range(8):
        column = lambda t: t[:, n : n + 1]
        for h, (sel, p, s, in_group, member) in enumerate((
            (sel0, pos0, slot0, rr // 16 == z, lax.rem(rr // 4, 4)),
            (sel1, pos1, slot1, lax.rem(rr // 4, 4) == y, rr // 16),
        )):
            on = column(sel) > 0
            here = on & in_group & (column(p) == lane)
            lists[h] = lists[h] + jnp.where(here, member * FIRST + column(s), 0)
            here = on & (rr // 4 == row) & (column(s) == lane)
            lists[2 + h] = lists[2 + h] + jnp.where(here, ids + n, 0)
    for n, t in enumerate(lists):
        ints[LISTS + n : LISTS + n + 1, :] = jnp.sum(t, axis=0, keepdims=True)

    i8, k8 = grid((8, 64))
    my_rows = one((k8 == row * 4 + i8) & (i8 < 4))
    floats[0:8, 0:64] = mm(my_rows, sp)
    floats[8:16, 0:8] = mm(mm(my_rows, ssq), mine)
    floats[16:24, 0:8] = mm(mm(my_rows, scb), mine)


def make_plan(pattern_p, pattern_sq, pattern_cube, placement, where=place, interpret=False):
    vmem = pl.BlockSpec(memory_space=pltpu.VMEM)
    return pl.pallas_call(
        functools.partial(plan_kernel, where),
        out_shape=(
            jax.ShapeDtypeStruct((ROWS, 128), jnp.int32),
            jax.ShapeDtypeStruct((24, 128), jnp.float32),
            jax.ShapeDtypeStruct((1, 1), jnp.int32),
        ),
        in_specs=[vmem] * 4,
        out_specs=(vmem, vmem, pl.BlockSpec(memory_space=pltpu.SMEM)),
        interpret=interpret,
    )(pattern_p, pattern_sq, pattern_cube, placement.reshape(1, 64))


def split(x):
    hi = x.astype(jnp.bfloat16)
    lo = (x - hi.astype(jnp.float32)).astype(jnp.bfloat16)
    return hi, lo


def product(left, right):
    lh, ll = split(left)
    rh, rl = split(right)
    lhs = jnp.concatenate([lh, lh, ll], axis=1)
    rhs = jnp.concatenate([rh, rl, rh], axis=0)
    return jnp.dot(lhs, rhs, preferred_element_type=jnp.float32)


class Ring:
    def __init__(self, part, size, me, plus, minus, ss, rs, base):
        up, down = lax.rem(me + 1, 4), lax.rem(me + 3, 4)
        cut = (size + 1) // 2
        own, left, right = part(me, 0, size), part(down, 0, size), part(up, 0, size)
        copy = lambda ref, n, dev: pltpu.make_async_remote_copy(
            src_ref=ref,
            dst_ref=ref,
            send_sem=ss.at[base + n],
            recv_sem=rs.at[base + n],
            device_id=dev,
            device_id_type=MESH,
        )
        self.copies = [
            copy(own, 0, plus),
            copy(own, 1, minus),
            copy(part(down, 0, cut), 2, plus),
            copy(part(up, cut, size - cut), 3, minus),
        ]

    def near(self):
        self.copies[0].start()
        self.copies[1].start()

    def far(self):
        self.copies[0].wait_recv()
        self.copies[2].start()
        self.copies[1].wait_recv()
        self.copies[3].start()

    def done(self):
        self.copies[2].wait_recv()
        self.copies[3].wait_recv()

    def sent(self):
        for c in self.copies:
            c.wait_send()


class Twin:
    def __init__(self, part, size, me, twin, ss, rs, base):
        self.copies = []
        for n in range(4):
            ref = part(lax.rem(me + n, 4), 0, size)
            self.copies.append(
                pltpu.make_async_remote_copy(
                    src_ref=ref,
                    dst_ref=ref,
                    send_sem=ss.at[base + n],
                    recv_sem=rs.at[base + n],
                    device_id=twin,
                    device_id_type=MESH,
                )
            )

    def start(self, *which):
        for n in which:
            self.copies[n].start()

    def recv(self, *which):
        for n in which:
            self.copies[n].wait_recv()

    def sent(self):
        for c in self.copies:
            c.wait_send()


COPIES = 8 + 8 + 4 * 8 + 4 * 8


def kernel(
    dens, ints, floats,
    out,
    a_buf, g0, g1, b0, b1, b2, b3, s2, s3, acc, ss, rs, own_sem,
):
    row, col = lax.axis_index("row"), lax.axis_index("col")
    z, y, x, core = row // 4, lax.rem(row, 4), col // 2, lax.rem(col, 2)
    up = lambda v: lax.rem(v + 1, 4)
    down = lambda v: lax.rem(v + 3, 4)
    yp, ym = (z * 4 + up(y), col), (z * 4 + down(y), col)
    zp, zm = (up(z) * 4 + y, col), (down(z) * 4 + y, col)
    xp, xm = (row, up(x) * 2 + core), (row, down(x) * 2 + core)
    twin = (row, x * 2 + 1 - core)
    pieces = (b0, b1, b2, b3)
    squares = (g0, g1, s2, s3)

    barrier = pltpu.get_barrier_semaphore()
    for dev in (yp, ym, zp, zm, xp, xm, twin):
        pl.semaphore_signal(barrier, inc=1, device_id=dev, device_id_type=MESH)

    mine = pltpu.make_async_copy(dens, a_buf.at[col], own_sem)
    mine.start()
    zero = jnp.zeros((BLOCK, BLOCK), jnp.float32)
    for piece, at in zip(pieces, ZERO):
        piece[at] = zero

    for i in range(4):
        for j in range(8):
            s2[i * 8 + j] = dens[i * BLOCK : (i + 1) * BLOCK, j * BLOCK : (j + 1) * BLOCK]

    def fill(s, _):
        g0[y * FIRST + s] = s2[ints[LISTS + 2, s]]
        g1[z * FIRST + s] = s2[ints[LISTS + 3, s]]
        return 0

    lax.fori_loop(0, FIRST, fill, 0)
    mine.wait()

    base = 0
    a_part = lambda m, lo, n: a_buf.at[m * 2 + core, pl.ds(lo, n)]
    a_ring = Ring(a_part, 512, x, xp, xm, ss, rs, base)
    a_twin = Twin(a_part, 512, x, twin, ss, rs, base + 4)
    base += 8
    g_rings = [
        Ring(lambda m, lo, n: g0.at[pl.ds(m * FIRST + lo, n)], FIRST, y, yp, ym, ss, rs, base),
        Ring(lambda m, lo, n: g1.at[pl.ds(m * FIRST + lo, n)], FIRST, z, zp, zm, ss, rs, base + 4),
    ]
    base += 8
    b_rings = []
    for piece, cap in zip(pieces, CAPS):
        part0 = lambda m, lo, n, r=piece, c=cap: r.at[pl.ds(m * c + lo, n)]
        part1 = lambda m, lo, n, r=piece, c=cap: r.at[pl.ds((4 + m) * c + lo, n)]
        b_rings.append([
            Ring(part0, cap, z, zp, zm, ss, rs, base),
            Ring(part1, cap, y, yp, ym, ss, rs, base + 4),
        ])
        base += 8
    s_rings, s_twins = [], []
    for sq in squares:
        part = lambda m, lo, n, r=sq: r.at[pl.ds((m * 2 + core) * 8 + lo, n)]
        s_rings.append(Ring(part, 8, x, xp, xm, ss, rs, base))
        s_twins.append(Twin(part, 8, x, twin, ss, rs, base + 4))
        base += 8

    near = lambda rings: [r.near() for r in rings]
    far = lambda rings: [r.far() for r in rings]
    done = lambda rings: [r.done() for r in rings]

    pl.semaphore_wait(barrier, 7)
    near(g_rings)
    a_ring.near()
    a_twin.start(0)
    far(g_rings)
    done(g_rings)

    for q in range(4):

        def regroup(s, _, q=q):
            pieces[q][z * CAPS[q] + s] = g0[ints[LISTS, STARTS[q] + s]]
            pieces[q][(4 + y) * CAPS[q] + s] = g1[ints[LISTS + 1, STARTS[q] + s]]
            return 0

        lax.fori_loop(0, CAPS[q], regroup, 0)
        if q < 2:
            near(b_rings[q])
    for r in g_rings:
        r.sent()

    def right_block(q, k, jj):
        block = pieces[q][ints[LOC + k, 8 + 2 * q + jj]]
        if q:
            block = block + pieces[q - 1][ints[LOC + k, 2 * q + jj]]
        return block

    def square(q):
        acc[...] = jnp.zeros_like(acc)

        def step(kk, _):
            k0 = kk * 4
            a = a_buf[kk // 2, :, pl.ds(pl.multiple_of(lax.rem(kk, 2) * 512, 512), 512)]
            left = jnp.concatenate([
                jnp.concatenate([
                    a[i * BLOCK : (i + 1) * BLOCK, t * BLOCK : (t + 1) * BLOCK] * floats[i, k0 + t]
                    for t in range(4)
                ], axis=1)
                for i in range(4)
            ], axis=0)
            right = jnp.concatenate([
                jnp.concatenate([right_block(q, k0 + t, jj) for jj in range(2)], axis=1)
                for t in range(4)
            ], axis=0)
            acc[...] += product(left, right)
            return 0

        lax.fori_loop(0, 16, step, 0)
        for i in range(4):
            for jj in range(2):
                squares[q][col * 8 + i * 2 + jj] = (
                    acc[i * BLOCK : (i + 1) * BLOCK, jj * BLOCK : (jj + 1) * BLOCK]
                    * floats[8 + i, 2 * q + jj]
                )
        s_rings[q].near()
        s_twins[q].start(0)

    def cube(q):
        def step(cd, _):
            left = jnp.concatenate([
                jnp.concatenate([squares[q][cd * 8 + i * 2 + t] for t in range(2)], axis=1)
                for i in range(4)
            ], axis=0)
            for n in range(4):
                right = jnp.concatenate([
                    jnp.concatenate([right_block(n, cd * 8 + 2 * q + t, jj) for jj in range(2)], axis=1)
                    for t in range(2)
                ], axis=0)
                out[:, n * 256 : (n + 1) * 256] += product(left, right)
            return 0

        lax.fori_loop(0, 8, step, 0)

    far(b_rings[0])
    near(b_rings[2])
    a_ring.far()
    a_twin.start(1, 3)
    done(b_rings[0])
    far(b_rings[1])
    near(b_rings[3])
    a_ring.done()
    a_twin.start(2)
    a_twin.recv(0, 1, 2, 3)
    square(0)
    done(b_rings[1])
    far(b_rings[2])
    square(1)
    s_rings[0].far()
    s_twins[0].start(1, 3)
    done(b_rings[2])
    far(b_rings[3])
    square(2)
    s_rings[0].done()
    s_twins[0].start(2)
    s_rings[1].far()
    s_twins[1].start(1, 3)
    out[...] = jnp.zeros_like(out)
    done(b_rings[3])
    square(3)
    s_rings[1].done()
    s_twins[1].start(2)
    s_rings[2].far()
    s_twins[2].start(1, 3)
    s_twins[0].recv(0, 1, 2, 3)
    cube(0)
    s_rings[2].done()
    s_twins[2].start(2)
    s_rings[3].far()
    s_twins[3].start(1, 3)
    s_twins[1].recv(0, 1, 2, 3)
    cube(1)
    s_rings[3].done()
    s_twins[3].start(2)
    s_twins[2].recv(0, 1, 2, 3)
    cube(2)
    s_twins[3].recv(0, 1, 2, 3)
    cube(3)
    for i in range(4):
        for q in range(4):
            for jj in range(2):
                j = 2 * q + jj
                at = (slice(i * BLOCK, (i + 1) * BLOCK), slice(j * BLOCK, (j + 1) * BLOCK))
                out[at] = 3.0 * squares[q][col * 8 + i * 2 + jj] - 2.0 * (out[at] * floats[16 + i, j])

    a_ring.sent()
    a_twin.sent()
    for pair in b_rings:
        for r in pair:
            r.sent()
    for r in s_rings + s_twins:
        r.sent()


def packed(density, ints, floats):
    smem = pl.BlockSpec(memory_space=pltpu.SMEM)
    vmem = pl.BlockSpec(memory_space=pltpu.VMEM)
    blocks = lambda n: pltpu.VMEM((n, BLOCK, BLOCK), jnp.float32)
    return pl.pallas_call(
        kernel,
        out_shape=jax.ShapeDtypeStruct(density.shape, jnp.float32),
        in_specs=[vmem, smem, smem],
        out_specs=vmem,
        scratch_shapes=[
            pltpu.VMEM((8, 512, 1024), jnp.float32),
            blocks(64),
            blocks(64),
            *[blocks(at + 1) for at in ZERO],
            blocks(64),
            blocks(64),
            pltpu.VMEM((512, 256), jnp.float32),
            pltpu.SemaphoreType.DMA((COPIES,)),
            pltpu.SemaphoreType.DMA((COPIES,)),
            pltpu.SemaphoreType.DMA,
        ],
        compiler_params=pltpu.CompilerParams(
            collective_id=0, has_side_effects=True, vmem_limit_bytes=62 * 2**20
        ),
        cost_estimate=pl.CostEstimate(flops=6 * 2**34, bytes_accessed=2**22, transcendentals=0),
    )(density, ints, floats)


def body(density, pattern_p, pattern_sq, pattern_cube, placement):
    ints, floats, fits = make_plan(pattern_p, pattern_sq, pattern_cube, placement)
    return lax.cond(
        fits[0, 0] > 0,
        lambda: packed(density, ints, floats),
        lambda: dense(density, pattern_p, pattern_sq, pattern_cube, placement),
    )


def solution(mesh):
    return jax.shard_map(
        body,
        mesh=mesh,
        in_specs=(P("row", "col"), P(), P(), P(), P()),
        out_specs=P("row", "col"),
        check_vma=False,
    )
```

```python
import functools

import jax
import jax.numpy as jnp
from jax import lax
from jax.experimental import pallas as pl
from jax.experimental.pallas import tpu as pltpu
from jax.sharding import PartitionSpec as P

BLOCK = 128
MESH = pl.DeviceIdType.MESH
CAPS = (12, 9, 9, 9)
ENDS = (12, 21, 30, 39)
STARTS = (0, 12, 21, 30)
ZERO = tuple(8 * cap for cap in CAPS)
FIRST = 12
PANEL = 24


def local_mask(stored, row_start, col_start, row_blocks, col_blocks):
    piece = lax.dynamic_slice(stored, (row_start, col_start), (row_blocks, col_blocks))
    return jnp.repeat(jnp.repeat(piece, BLOCK, axis=0), BLOCK, axis=1)


def dense(density, pattern_p, pattern_sq, pattern_cube, placement):
    count = pattern_p.shape[0]
    row_blocks = density.shape[0] // BLOCK
    col_blocks = density.shape[1] // BLOCK
    row_start = lax.axis_index("row") * row_blocks
    col_start = lax.axis_index("col") * col_blocks
    onehot = (placement[:, None] == jnp.arange(count, dtype=jnp.int32)[None, :]).astype(jnp.float32)

    def stored(pattern):
        moved = jnp.dot(onehot.T, pattern.astype(jnp.float32), precision=lax.Precision.HIGHEST)
        return jnp.dot(moved, onehot, precision=lax.Precision.HIGHEST)

    stored_p, stored_sq, stored_cube = (stored(p) for p in (pattern_p, pattern_sq, pattern_cube))
    kept = density * local_mask(stored_p, row_start, col_start, row_blocks, col_blocks)
    mask_sq = local_mask(stored_sq, row_start, col_start, row_blocks, col_blocks)
    mask_cube = local_mask(stored_cube, row_start, col_start, row_blocks, col_blocks)
    kept_panel = lax.all_gather(kept, "col", axis=1, tiled=True)
    columns = lax.all_gather(kept, "row", axis=0, tiled=True)
    square = jnp.dot(kept_panel, columns, precision=lax.Precision.HIGHEST) * mask_sq
    square_panel = lax.all_gather(square, "col", axis=1, tiled=True)
    cube = jnp.dot(square_panel, columns, precision=lax.Precision.HIGHEST) * mask_cube
    return 3.0 * square - 2.0 * cube


LOC, LISTS, LEFT, ROWS = 0, 64, 72, 80


def place():
    return lax.axis_index("row"), lax.axis_index("col")


def plan_kernel(where, pat_p, pat_sq, pat_cube, placement, ints, floats, fits):
    row, col = where()
    z, y, x, core = row // 4, lax.rem(row, 4), col // 2, lax.rem(col, 2)
    f32, bf16 = jnp.float32, jnp.bfloat16

    def grid(shape):
        return lax.broadcasted_iota(jnp.int32, shape, 0), lax.broadcasted_iota(jnp.int32, shape, 1)

    def mm(*terms):
        out = terms[0]
        for t in terms[1:]:
            out = jnp.dot(out.astype(bf16), t.astype(bf16), preferred_element_type=f32)
        return out

    def one(cond):
        return jnp.where(cond, 1.0, 0.0).astype(f32)

    a, b = grid((64, 64))
    onehot_t = one(placement[...] == a)

    def stored(pattern):
        moved = mm(onehot_t, pattern[...].astype(f32))
        return lax.dot_general(
            moved.astype(bf16), onehot_t.astype(bf16), (((1,), (1,)), ((), ())), preferred_element_type=f32
        )

    sp, ssq, scb = stored(pat_p), stored(pat_sq), stored(pat_cube)

    d, k = grid((16, 64))
    device_rows = one(k // 4 == d)
    k2, d2 = grid((64, 16))
    rows_device = one(k2 // 4 == d2)
    j, c = grid((64, 8))
    c2, j2 = grid((8, 64))
    pair = [one((j // 8 == c) & (lax.rem(j, 8) // 2 == q)) for q in range(4)]
    pair_t = [one((j2 // 8 == c2) & (lax.rem(j2, 8) // 2 == q)) for q in range(4)]
    same_pair = one(a // 2 == b // 2)
    pair_before = one((a // 2 == b // 2) & (a < b))
    chip_before = one((a // 16 == b // 16) & (a < b))
    chip = one(a // 16 == b // 16)
    device = a // 4 == b // 4
    rows_before = one(device & (b < a))
    d3, d4 = grid((16, 16))
    mean = (one(lax.rem(d3, 4) == lax.rem(d4, 4)) - one(d3 // 4 == d4 // 4)) * 0.125
    dd, _ = grid((16, 8))
    dither = (lax.rem(dd // 4 + lax.rem(dd, 4), 2)).astype(f32) * 0.5 + 0.25

    by_device = mm(device_rows, sp)
    total = jnp.zeros((16, 8), f32)
    have = jnp.zeros((16, 8), f32)
    share = jnp.zeros((64, 64), f32)
    for q in range(4):
        n = mm(by_device, pair[q])
        total = total + n
        target = jnp.floor(total * 0.5 + mm(mean, total) + dither)
        inc = jnp.minimum(jnp.maximum(target - have, 0.0), n)
        have = have + inc
        share = share + mm(mm(rows_device, inc), pair_t[q])
    worst = jnp.float32(0.0)

    rank = mm(mm(rows_before, sp), same_pair) + mm(sp, pair_before)
    first = sp * one(rank < share)
    second = sp - first

    routes = []
    for sel, group_of in ((first, lambda r: r // 16), (second, lambda r: lax.rem(r // 4, 4))):
        g, kk = grid((8, 64))
        group_rows = one(group_of(kk) == g)
        kk2, g2 = grid((64, 8))
        rows_group = one(group_of(kk2) == g2)
        by_group = mm(group_rows, sel)
        start = jnp.zeros((8, 8), f32)
        base = jnp.zeros((64, 64), f32)
        for q in range(4):
            start = jnp.maximum(start, float(STARTS[max(q - 1, 0)]))
            base = base + mm(mm(rows_group, start), pair_t[q])
            start = start + mm(by_group, pair[q])
            worst = jnp.maximum(worst, jnp.max(start - ENDS[q]))
        order = one((group_of(a) == group_of(b)) & (b < a))
        in_pair = mm(sel, pair_before)
        pos = base + mm(mm(order, sel), same_pair) + in_pair
        turn = mm(mm(rows_before, sel), chip) + mm(sel, chip_before)
        worst = jnp.maximum(worst, jnp.max(sel * (turn + (1.0 - 2.0 * FIRST))))
        slot = jnp.floor(turn * 0.5)
        routes.append((pos, (turn - 2.0 * slot) * FIRST + slot, turn))
    turn = mm(mm(rows_before, sp), chip) + mm(sp, chip_before)
    worst = jnp.maximum(worst, jnp.max(sp * (turn + (1.0 - 2.0 * PANEL))))
    i8, k8 = grid((8, 64))
    my_rows = one((k8 == row * 4 + i8) & (i8 < 4))
    my_turn, my_kept = mm(my_rows, turn), mm(my_rows, sp)
    order = my_turn.astype(jnp.int32)
    at = (k8 // 16 * 2 + lax.rem(order, 2)) * PANEL + order // 2
    ints[LEFT : LEFT + 8, 0:64] = jnp.where(my_kept > 0, at, 8 * PANEL)
    m16, n16 = grid((64, 16))
    chip_columns = one((m16 // 16 == x) & (lax.rem(m16, 16) == n16))
    i_lane, lane8 = grid((8, 128))
    for at, kept, turn in ((2, first, routes[0][2]), (3, second, routes[1][2]), (4, sp, turn)):
        order = mm(my_rows, turn, chip_columns).astype(jnp.int32)
        on = mm(my_rows, kept, chip_columns) > 0
        take = jnp.zeros((8, 128), jnp.int32)
        for n in range(16):
            this = order[:, n : n + 1]
            here = on[:, n : n + 1] & (lax.rem(this, 2) == core) & (this // 2 == lane8)
            take = take + jnp.where(here, (n // 8) * 32 + i_lane * 8 + n % 8, 0)
        ints[LISTS + at : LISTS + at + 1, :] = jnp.sum(take, axis=0, keepdims=True)
    fits[0, 0] = jnp.where(worst <= 0.0, 1, 0)

    mine = one((j // 8 == col) & (lax.rem(j, 8) == c))
    panel = lambda t: mm(t, mine).astype(jnp.int32)
    sel0, sel1 = panel(first), panel(second)
    pos0, pos1 = panel(routes[0][0]), panel(routes[1][0])
    slot0, slot1 = panel(routes[0][1]), panel(routes[1][1])
    r, jl = grid((64, 8))
    pos = jnp.where(sel0 > 0, pos0, pos1)
    group = jnp.where(sel0 > 0, r // 16, 4 + lax.rem(r // 4, 4))
    there = (sel0 + sel1) > 0
    q = jl // 2
    table = lambda values: sum(jnp.where(q == n, v, 0) for n, v in enumerate(values))
    early = tuple(max(n - 1, 0) for n in range(4))
    late = pos >= table(STARTS)
    cur = jnp.where(there & late, group * table(CAPS) + pos - table(STARTS), table(ZERO))
    prev_caps = table([CAPS[p] for p in early])
    prev_start = table([STARTS[p] for p in early])
    prev_zero = table([ZERO[p] for p in early])
    prev = jnp.where(there & ~late, group * prev_caps + pos - prev_start, prev_zero)
    ints[LOC : LOC + 64, 0:8] = prev
    ints[LOC : LOC + 64, 8:16] = cur

    rr, lane = grid((64, 128))
    lists = [jnp.zeros((64, 128), jnp.int32) for _ in range(2)]
    for n in range(8):
        column = lambda t: t[:, n : n + 1]
        for h, (sel, p, s, in_group, member) in enumerate((
            (sel0, pos0, slot0, rr // 16 == z, lax.rem(rr // 4, 4)),
            (sel1, pos1, slot1, lax.rem(rr // 4, 4) == y, rr // 16),
        )):
            on = column(sel) > 0
            here = on & in_group & (column(p) == lane)
            lists[h] = lists[h] + jnp.where(here, member * 2 * FIRST + column(s), 0)
    for n, t in enumerate(lists):
        ints[LISTS + n : LISTS + n + 1, :] = jnp.sum(t, axis=0, keepdims=True)

    floats[0:8, 0:8] = mm(mm(my_rows, ssq), mine)
    floats[8:16, 0:8] = mm(mm(my_rows, scb), mine)


def make_plan(pattern_p, pattern_sq, pattern_cube, placement, where=place, interpret=False):
    vmem = pl.BlockSpec(memory_space=pltpu.VMEM)
    return pl.pallas_call(
        functools.partial(plan_kernel, where),
        out_shape=(
            jax.ShapeDtypeStruct((ROWS, 128), jnp.int32),
            jax.ShapeDtypeStruct((16, 128), jnp.float32),
            jax.ShapeDtypeStruct((1, 1), jnp.int32),
        ),
        in_specs=[vmem] * 4,
        out_specs=(vmem, vmem, pl.BlockSpec(memory_space=pltpu.SMEM)),
        interpret=interpret,
    )(pattern_p, pattern_sq, pattern_cube, placement.reshape(1, 64))


def split(x):
    hi = x.astype(jnp.bfloat16)
    lo = (x - hi.astype(jnp.float32)).astype(jnp.bfloat16)
    return hi, lo


def product(left, right):
    lh, ll = left
    rh, rl = split(right)
    lhs = jnp.concatenate([lh, lh, ll], axis=1)
    rhs = jnp.concatenate([rh, rl, rh], axis=0)
    return jnp.dot(lhs, rhs, preferred_element_type=jnp.float32)


class Ring:
    def __init__(self, part, size, me, plus, minus, ss, rs, base):
        up, down = lax.rem(me + 1, 4), lax.rem(me + 3, 4)
        cut = (size + 1) // 2
        own, left, right = part(me, 0, size), part(down, 0, size), part(up, 0, size)
        copy = lambda ref, n, dev: pltpu.make_async_remote_copy(
            src_ref=ref,
            dst_ref=ref,
            send_sem=ss.at[base + n],
            recv_sem=rs.at[base + n],
            device_id=dev,
            device_id_type=MESH,
        )
        self.copies = [
            copy(own, 0, plus),
            copy(own, 1, minus),
            copy(part(down, 0, cut), 2, plus),
            copy(part(up, cut, size - cut), 3, minus),
        ]

    def near(self):
        self.copies[0].start()
        self.copies[1].start()

    def far(self):
        self.copies[0].wait_recv()
        self.copies[2].start()
        self.copies[1].wait_recv()
        self.copies[3].start()

    def done(self):
        self.copies[2].wait_recv()
        self.copies[3].wait_recv()

    def sent(self):
        for c in self.copies:
            c.wait_send()


class Twin:
    def __init__(self, part, size, me, twin, ss, rs, base):
        self.copies = []
        for n in range(4):
            ref = part(lax.rem(me + n, 4), 0, size)
            self.copies.append(
                pltpu.make_async_remote_copy(
                    src_ref=ref,
                    dst_ref=ref,
                    send_sem=ss.at[base + n],
                    recv_sem=rs.at[base + n],
                    device_id=twin,
                    device_id_type=MESH,
                )
            )

    def start(self, *which):
        for n in which:
            self.copies[n].start()

    def recv(self, *which):
        for n in which:
            self.copies[n].wait_recv()

    def sent(self):
        for c in self.copies:
            c.wait_send()


COPIES = 16 + 16 + 4 * 8 + 5 * 8 + 1


def kernel(
    dens, ints, floats,
    out,
    a_buf, a_hi, a_lo, g0, g1, b0, b1, b2, b3, acc, ss, rs, own_sem,
):
    row, col = lax.axis_index("row"), lax.axis_index("col")
    z, y, x, core = row // 4, lax.rem(row, 4), col // 2, lax.rem(col, 2)
    up = lambda v: lax.rem(v + 1, 4)
    down = lambda v: lax.rem(v + 3, 4)
    yp, ym = (z * 4 + up(y), col), (z * 4 + down(y), col)
    zp, zm = (up(z) * 4 + y, col), (down(z) * 4 + y, col)
    xp, xm = (row, up(x) * 2 + core), (row, down(x) * 2 + core)
    twin = (row, x * 2 + 1 - core)
    pieces = (b0, b1, b2, b3)
    squares = ((g0, 0), (g1, 0), (a_buf, 0), (a_buf, 64))

    barrier = pltpu.get_barrier_semaphore()
    for dev in (yp, ym, zp, zm, xp, xm, twin):
        pl.semaphore_signal(barrier, inc=1, device_id=dev, device_id_type=MESH)

    def fetch(n, _):
        block = dens.at[
            pl.ds(pl.multiple_of(n // 8 * BLOCK, BLOCK), BLOCK),
            pl.ds(pl.multiple_of(lax.rem(n, 8) * BLOCK, BLOCK), BLOCK),
        ]
        pltpu.make_async_copy(block, b0.at[core * 32 + n], own_sem).start()
        return 0

    lax.fori_loop(0, 32, fetch, 0)
    zero = jnp.zeros((BLOCK, BLOCK), jnp.float32)
    for piece, at in zip(pieces, ZERO):
        piece[at] = zero
    a_buf[8 * PANEL] = zero

    base = 0
    half = PANEL // 2
    a_rings, a_twins = [], []
    for p in range(2):
        part = lambda m, lo, n, p=p: a_buf.at[pl.ds((m * 2 + core) * PANEL + p * half + lo, n)]
        a_rings.append(Ring(part, half, x, xp, xm, ss, rs, base))
        a_twins.append(Twin(part, half, x, twin, ss, rs, base + 4))
        base += 8
    g_rings, g_twins = [], []
    for ref, me, plus, minus in ((g0, y, yp, ym), (g1, z, zp, zm)):
        part = lambda m, lo, n, r=ref: r.at[pl.ds((m * 2 + core) * FIRST + lo, n)]
        g_rings.append(Ring(part, FIRST, me, plus, minus, ss, rs, base))
        g_twins.append(Twin(part, FIRST, me, twin, ss, rs, base + 4))
        base += 8
    b_rings = []
    for piece, cap in zip(pieces, CAPS):
        part0 = lambda m, lo, n, r=piece, c=cap: r.at[pl.ds(m * c + lo, n)]
        part1 = lambda m, lo, n, r=piece, c=cap: r.at[pl.ds((4 + m) * c + lo, n)]
        b_rings.append([
            Ring(part0, cap, z, zp, zm, ss, rs, base),
            Ring(part1, cap, y, yp, ym, ss, rs, base + 4),
        ])
        base += 8
    s_rings, s_twins = [], []
    for q, (ref, off) in enumerate(squares):
        s_rings.append([])
        s_twins.append([])
        parts = 2 if q == 3 else 1
        size = 8 // parts
        for p in range(parts):
            part = lambda m, lo, n, r=ref, o=off + p * size: r.at[pl.ds(o + (m * 2 + core) * 8 + lo, n)]
            s_rings[q].append(Ring(part, size, x, xp, xm, ss, rs, base))
            s_twins[q].append(Twin(part, size, x, twin, ss, rs, base + 4))
            base += 8
    raw = pltpu.make_async_remote_copy(
        src_ref=b0.at[pl.ds(core * 32, 32)],
        dst_ref=b0.at[pl.ds(core * 32, 32)],
        send_sem=ss.at[base],
        recv_sem=rs.at[base],
        device_id=twin,
        device_id_type=MESH,
    )

    near = lambda rings: [r.near() for r in rings]
    far = lambda rings: [r.far() for r in rings]
    done = lambda rings: [r.done() for r in rings]

    own = b0.at[pl.ds(core * 32, 32)]
    pltpu.make_async_copy(own, own, own_sem).wait()
    pl.semaphore_wait(barrier, 7)
    raw.start()
    raw.wait()

    def fill(s, _):
        g0[(y * 2 + core) * FIRST + s] = b0[ints[LISTS + 2, s]]
        g1[(z * 2 + core) * FIRST + s] = b0[ints[LISTS + 3, s]]
        return 0

    def panel(s, _):
        a_buf[col * PANEL + s] = b0[ints[LISTS + 4, s]]
        return 0

    lax.fori_loop(0, FIRST, fill, 0)
    lax.fori_loop(0, PANEL, panel, 0)
    near(g_rings)
    for t in g_twins:
        t.start(0)
    for p in range(2):
        a_rings[p].near()
        a_twins[p].start(0)
    far(g_rings)
    for t in g_twins:
        t.start(1, 3)
    done(g_rings)
    for t in g_twins:
        t.start(2)
    for t in g_twins:
        t.recv(0, 1, 2, 3)

    for q in range(4):

        def regroup(s, _, q=q):
            pieces[q][z * CAPS[q] + s] = g0[ints[LISTS, STARTS[q] + s]]
            pieces[q][(4 + y) * CAPS[q] + s] = g1[ints[LISTS + 1, STARTS[q] + s]]
            return 0

        lax.fori_loop(0, CAPS[q], regroup, 0)
        if q == 0:
            near(b_rings[q])
    for r in g_rings + g_twins:
        r.sent()

    def right_block(q, k, jj):
        block = pieces[q][ints[LOC + k, 8 + 2 * q + jj]]
        if q:
            block = block + pieces[q - 1][ints[LOC + k, 2 * q + jj]]
        return block

    def square(q, rows, lo, hi):
        tall = len(rows) * BLOCK

        def step(kk, _):
            k0 = kk * 4
            left = [
                jnp.concatenate([
                    jnp.concatenate([a[ints[LEFT + i, k0 + t]] for t in range(4)], axis=1)
                    for i in rows
                ], axis=0)
                for a in (a_hi, a_lo)
            ]
            right = jnp.concatenate([
                jnp.concatenate([right_block(q, k0 + t, jj) for jj in range(2)], axis=1)
                for t in range(4)
            ], axis=0)
            acc[0:tall, :] += product(left, right)
            return 0

        if lo == 0:
            acc[...] = jnp.zeros_like(acc)
        lax.fori_loop(lo, hi, step, 0)

    def send_square(q, rows, part):
        ref, off = squares[q]
        for n, i in enumerate(rows):
            for jj in range(2):
                ref[off + col * 8 + i * 2 + jj] = (
                    acc[n * BLOCK : (n + 1) * BLOCK, jj * BLOCK : (jj + 1) * BLOCK]
                    * floats[i, 2 * q + jj]
                )
        s_rings[q][part].near()
        s_twins[q][part].start(0)

    def cube(q, pairs, lo=0, hi=4):
        ref, off = squares[q]

        def step(o, _):
            o = o + jnp.where(o == 2, 1, 0) - jnp.where(o == 3, 1, 0)
            cd = lax.rem(x + o, 4) * 2
            left = split(jnp.concatenate([
                jnp.concatenate([ref[off + (cd + t // 2) * 8 + i * 2 + t % 2] for t in range(4)], axis=1)
                for i in range(4)
            ], axis=0))
            for n in pairs:
                right = jnp.concatenate([
                    jnp.concatenate([right_block(n, (cd + t // 2) * 8 + 2 * q + t % 2, jj) for jj in range(2)], axis=1)
                    for t in range(4)
                ], axis=0)
                out[:, n * 256 : (n + 1) * 256] += product(left, right)
            return 0

        lax.fori_loop(lo, hi, step, 0)

    def s_far(q):
        for r, t in zip(s_rings[q], s_twins[q]):
            r.far()
            t.start(1, 3)

    def s_done(q):
        for r, t in zip(s_rings[q], s_twins[q]):
            r.done()
            t.start(2)

    def s_recv(q, *which):
        for t in s_twins[q]:
            t.recv(*which)

    every, top, bottom = range(4), range(2), range(2, 4)
    for p in range(2):
        a_rings[p].far()
        a_twins[p].start(1, 3)
    far(b_rings[0])
    near(b_rings[1])
    for p in range(2):
        a_rings[p].done()
        a_twins[p].start(2)
    for p in range(2):
        a_twins[p].recv(0, 1, 2, 3)

    def cut(n, _):
        a_hi[n], a_lo[n] = split(a_buf[n])
        return 0

    lax.fori_loop(0, 8 * PANEL + 1, cut, 0)
    for r in a_rings + a_twins:
        r.sent()
    out[...] = jnp.zeros_like(out)
    done(b_rings[0])
    square(0, every, 0, 16)
    send_square(0, every, 0)
    far(b_rings[1])
    near(b_rings[2])
    done(b_rings[1])
    square(1, every, 0, 8)
    s_far(0)
    square(1, every, 8, 16)
    send_square(1, every, 0)
    far(b_rings[2])
    near(b_rings[3])
    s_done(0)
    s_recv(0, 0, 1, 2, 3)
    cube(0, (0, 1))
    done(b_rings[2])
    square(2, every, 0, 8)
    s_far(1)
    square(2, every, 8, 16)
    send_square(2, every, 0)
    cube(0, (2,))
    far(b_rings[3])
    s_done(1)
    s_recv(1, 0, 1, 2, 3)
    cube(1, (0, 1, 2))
    done(b_rings[3])
    square(3, top, 0, 16)
    s_far(2)
    send_square(3, top, 0)
    square(3, bottom, 0, 16)
    send_square(3, bottom, 1)
    cube(0, (3,))
    cube(1, (3,))
    s_done(2)
    s_far(3)
    s_recv(2, 0, 1, 2, 3)
    cube(2, (0, 1, 2, 3))
    s_done(3)
    s_recv(3, 0, 1, 3)
    cube(3, (0, 1, 2, 3), 0, 3)
    s_recv(3, 2)
    cube(3, (0, 1, 2, 3), 3, 4)
    for i in range(4):
        for q in range(4):
            for jj in range(2):
                j = 2 * q + jj
                at = (slice(i * BLOCK, (i + 1) * BLOCK), slice(j * BLOCK, (j + 1) * BLOCK))
                out[at] = 3.0 * squares[q][0][squares[q][1] + col * 8 + i * 2 + jj] - 2.0 * (out[at] * floats[8 + i, j])

    for pair in b_rings:
        for r in pair:
            r.sent()
    for parts in s_rings + s_twins:
        for r in parts:
            r.sent()


def packed(density, ints, floats):
    smem = pl.BlockSpec(memory_space=pltpu.SMEM)
    vmem = pl.BlockSpec(memory_space=pltpu.VMEM)
    blocks = lambda n: pltpu.VMEM((n, BLOCK, BLOCK), jnp.float32)
    return pl.pallas_call(
        kernel,
        out_shape=jax.ShapeDtypeStruct(density.shape, jnp.float32),
        in_specs=[pl.BlockSpec(memory_space=pl.ANY), smem, smem],
        out_specs=vmem,
        scratch_shapes=[
            blocks(8 * PANEL + 1),
            pltpu.VMEM((8 * PANEL + 1, BLOCK, BLOCK), jnp.bfloat16),
            pltpu.VMEM((8 * PANEL + 1, BLOCK, BLOCK), jnp.bfloat16),
            blocks(8 * FIRST),
            blocks(8 * FIRST),
            *[blocks(at + 1) for at in ZERO],
            pltpu.VMEM((512, 256), jnp.float32),
            pltpu.SemaphoreType.DMA((COPIES,)),
            pltpu.SemaphoreType.DMA((COPIES,)),
            pltpu.SemaphoreType.DMA,
        ],
        compiler_params=pltpu.CompilerParams(
            collective_id=0, has_side_effects=True, vmem_limit_bytes=127 * 2**19
        ),
        cost_estimate=pl.CostEstimate(flops=6 * 2**34, bytes_accessed=2**22, transcendentals=0),
    )(density, ints, floats)


def body(density, pattern_p, pattern_sq, pattern_cube, placement):
    ints, floats, fits = make_plan(pattern_p, pattern_sq, pattern_cube, placement)
    return lax.cond(
        fits[0, 0] > 0,
        lambda: packed(density, ints, floats),
        lambda: dense(density, pattern_p, pattern_sq, pattern_cube, placement),
    )


def solution(mesh):
    return jax.shard_map(
        body,
        mesh=mesh,
        in_specs=(P("row", "col"), P(), P(), P(), P()),
        out_specs=P("row", "col"),
        check_vma=False,
    )
```

```python
import functools

import jax
import jax.numpy as jnp
from jax import lax
from jax.experimental import pallas as pl
from jax.experimental.pallas import tpu as pltpu
from jax.sharding import PartitionSpec as P

BLOCK = 128
MESH = pl.DeviceIdType.MESH
CAPS = (12, 9, 9, 9)
ENDS = (12, 21, 30, 39)
STARTS = (0, 12, 21, 30)
ZERO = tuple(8 * cap for cap in CAPS)
FIRST = 12
PANEL = 24


def local_mask(stored, row_start, col_start, row_blocks, col_blocks):
    piece = lax.dynamic_slice(stored, (row_start, col_start), (row_blocks, col_blocks))
    return jnp.repeat(jnp.repeat(piece, BLOCK, axis=0), BLOCK, axis=1)


def dense(density, pattern_p, pattern_sq, pattern_cube, placement):
    count = pattern_p.shape[0]
    row_blocks = density.shape[0] // BLOCK
    col_blocks = density.shape[1] // BLOCK
    row_start = lax.axis_index("row") * row_blocks
    col_start = lax.axis_index("col") * col_blocks
    onehot = (placement[:, None] == jnp.arange(count, dtype=jnp.int32)[None, :]).astype(jnp.float32)

    def stored(pattern):
        moved = jnp.dot(onehot.T, pattern.astype(jnp.float32), precision=lax.Precision.HIGHEST)
        return jnp.dot(moved, onehot, precision=lax.Precision.HIGHEST)

    stored_p, stored_sq, stored_cube = (stored(p) for p in (pattern_p, pattern_sq, pattern_cube))
    kept = density * local_mask(stored_p, row_start, col_start, row_blocks, col_blocks)
    mask_sq = local_mask(stored_sq, row_start, col_start, row_blocks, col_blocks)
    mask_cube = local_mask(stored_cube, row_start, col_start, row_blocks, col_blocks)
    columns = lax.all_gather(kept, "row", axis=0, tiled=True)

    def step(left, mask):
        panel = lax.all_gather(left, "col", axis=1, tiled=True)
        product = jnp.dot(panel, columns, precision=lax.Precision.HIGH) * mask
        return product, product

    _, (square, cube) = lax.scan(step, kept, jnp.stack([mask_sq, mask_cube]))
    return 3.0 * square - 2.0 * cube


LOC, LISTS, LEFT, ROWS = 0, 64, 72, 80


def place():
    return lax.axis_index("row"), lax.axis_index("col")


def plan_kernel(where, pat_p, pat_sq, pat_cube, placement, ints, floats, fits):
    row, col = where()
    z, y, x, core = row // 4, lax.rem(row, 4), col // 2, lax.rem(col, 2)
    f32, bf16 = jnp.float32, jnp.bfloat16

    def grid(shape):
        return lax.broadcasted_iota(jnp.int32, shape, 0), lax.broadcasted_iota(jnp.int32, shape, 1)

    def mm(*terms):
        out = terms[0]
        for t in terms[1:]:
            out = jnp.dot(out.astype(bf16), t.astype(bf16), preferred_element_type=f32)
        return out

    def one(cond):
        return jnp.where(cond, 1.0, 0.0).astype(f32)

    a, b = grid((64, 64))
    onehot_t = one(placement[...] == a)

    def stored(pattern):
        moved = mm(onehot_t, pattern[...].astype(f32))
        return lax.dot_general(
            moved.astype(bf16), onehot_t.astype(bf16), (((1,), (1,)), ((), ())), preferred_element_type=f32
        )

    sp, ssq, scb = stored(pat_p), stored(pat_sq), stored(pat_cube)

    d, k = grid((16, 64))
    device_rows = one(k // 4 == d)
    k2, d2 = grid((64, 16))
    rows_device = one(k2 // 4 == d2)
    j, c = grid((64, 8))
    c2, j2 = grid((8, 64))
    pair = [one((j // 8 == c) & (lax.rem(j, 8) // 2 == q)) for q in range(4)]
    pair_t = [one((j2 // 8 == c2) & (lax.rem(j2, 8) // 2 == q)) for q in range(4)]
    same_pair = one(a // 2 == b // 2)
    pair_before = one((a // 2 == b // 2) & (a < b))
    chip_before = one((a // 16 == b // 16) & (a < b))
    chip = one(a // 16 == b // 16)
    device = a // 4 == b // 4
    rows_before = one(device & (b < a))
    d3, d4 = grid((16, 16))
    mean = (one(lax.rem(d3, 4) == lax.rem(d4, 4)) - one(d3 // 4 == d4 // 4)) * 0.125
    dd, _ = grid((16, 8))
    dither = (lax.rem(dd // 4 + lax.rem(dd, 4), 2)).astype(f32) * 0.5 + 0.25

    by_device = mm(device_rows, sp)
    total = jnp.zeros((16, 8), f32)
    have = jnp.zeros((16, 8), f32)
    share = jnp.zeros((64, 64), f32)
    for q in range(4):
        n = mm(by_device, pair[q])
        total = total + n
        target = jnp.floor(total * 0.5 + mm(mean, total) + dither)
        inc = jnp.minimum(jnp.maximum(target - have, 0.0), n)
        have = have + inc
        share = share + mm(mm(rows_device, inc), pair_t[q])
    worst = jnp.float32(0.0)

    rank = mm(mm(rows_before, sp), same_pair) + mm(sp, pair_before)
    first = sp * one(rank < share)
    second = sp - first

    routes = []
    for sel, group_of in ((first, lambda r: r // 16), (second, lambda r: lax.rem(r // 4, 4))):
        g, kk = grid((8, 64))
        group_rows = one(group_of(kk) == g)
        kk2, g2 = grid((64, 8))
        rows_group = one(group_of(kk2) == g2)
        by_group = mm(group_rows, sel)
        start = jnp.zeros((8, 8), f32)
        base = jnp.zeros((64, 64), f32)
        for q in range(4):
            start = jnp.maximum(start, float(STARTS[max(q - 1, 0)]))
            base = base + mm(mm(rows_group, start), pair_t[q])
            start = start + mm(by_group, pair[q])
            worst = jnp.maximum(worst, jnp.max(start - ENDS[q]))
        order = one((group_of(a) == group_of(b)) & (b < a))
        in_pair = mm(sel, pair_before)
        pos = base + mm(mm(order, sel), same_pair) + in_pair
        turn = mm(mm(rows_before, sel), chip) + mm(sel, chip_before)
        worst = jnp.maximum(worst, jnp.max(sel * (turn + (1.0 - 2.0 * FIRST))))
        slot = jnp.floor(turn * 0.5)
        routes.append((pos, (turn - 2.0 * slot) * FIRST + slot, turn))
    turn = mm(mm(rows_before, sp), chip) + mm(sp, chip_before)
    worst = jnp.maximum(worst, jnp.max(sp * (turn + (1.0 - 2.0 * PANEL))))
    i8, k8 = grid((8, 64))
    my_rows = one((k8 == row * 4 + i8) & (i8 < 4))
    my_turn, my_kept = mm(my_rows, turn), mm(my_rows, sp)
    order = my_turn.astype(jnp.int32)
    at = (k8 // 16 * 2 + lax.rem(order, 2)) * PANEL + order // 2
    ints[LEFT : LEFT + 8, 0:64] = jnp.where(my_kept > 0, at, 8 * PANEL)
    m16, n16 = grid((64, 16))
    chip_columns = one((m16 // 16 == x) & (lax.rem(m16, 16) == n16))
    i_lane, lane8 = grid((8, 128))
    for at, kept, turn in ((2, first, routes[0][2]), (3, second, routes[1][2]), (4, sp, turn)):
        order = mm(my_rows, turn, chip_columns).astype(jnp.int32)
        on = mm(my_rows, kept, chip_columns) > 0
        take = jnp.zeros((8, 128), jnp.int32)
        for n in range(16):
            this = order[:, n : n + 1]
            here = on[:, n : n + 1] & (lax.rem(this, 2) == core) & (this // 2 == lane8)
            take = take + jnp.where(here, (n // 8) * 32 + i_lane * 8 + n % 8, 0)
        ints[LISTS + at : LISTS + at + 1, :] = jnp.sum(take, axis=0, keepdims=True)
    fits[0, 0] = jnp.where(worst <= 0.0, 1, 0)

    mine = one((j // 8 == col) & (lax.rem(j, 8) == c))
    panel = lambda t: mm(t, mine).astype(jnp.int32)
    sel0, sel1 = panel(first), panel(second)
    pos0, pos1 = panel(routes[0][0]), panel(routes[1][0])
    slot0, slot1 = panel(routes[0][1]), panel(routes[1][1])
    r, jl = grid((64, 8))
    pos = jnp.where(sel0 > 0, pos0, pos1)
    group = jnp.where(sel0 > 0, r // 16, 4 + lax.rem(r // 4, 4))
    there = (sel0 + sel1) > 0
    q = jl // 2
    table = lambda values: sum(jnp.where(q == n, v, 0) for n, v in enumerate(values))
    early = tuple(max(n - 1, 0) for n in range(4))
    late = pos >= table(STARTS)
    cur = jnp.where(there & late, group * table(CAPS) + pos - table(STARTS), table(ZERO))
    prev_caps = table([CAPS[p] for p in early])
    prev_start = table([STARTS[p] for p in early])
    prev_zero = table([ZERO[p] for p in early])
    prev = jnp.where(there & ~late, group * prev_caps + pos - prev_start, prev_zero)
    ints[LOC : LOC + 64, 0:8] = prev
    ints[LOC : LOC + 64, 8:16] = cur

    rr, lane = grid((64, 128))
    lists = [jnp.zeros((64, 128), jnp.int32) for _ in range(2)]
    for n in range(8):
        column = lambda t: t[:, n : n + 1]
        for h, (sel, p, s, in_group, member) in enumerate((
            (sel0, pos0, slot0, rr // 16 == z, lax.rem(rr // 4, 4)),
            (sel1, pos1, slot1, lax.rem(rr // 4, 4) == y, rr // 16),
        )):
            on = column(sel) > 0
            here = on & in_group & (column(p) == lane)
            lists[h] = lists[h] + jnp.where(here, member * 2 * FIRST + column(s), 0)
    for n, t in enumerate(lists):
        ints[LISTS + n : LISTS + n + 1, :] = jnp.sum(t, axis=0, keepdims=True)

    floats[0:8, 0:8] = mm(mm(my_rows, ssq), mine)
    floats[8:16, 0:8] = mm(mm(my_rows, scb), mine)


def make_plan(pattern_p, pattern_sq, pattern_cube, placement, where=place, interpret=False):
    vmem = pl.BlockSpec(memory_space=pltpu.VMEM)
    return pl.pallas_call(
        functools.partial(plan_kernel, where),
        out_shape=(
            jax.ShapeDtypeStruct((ROWS, 128), jnp.int32),
            jax.ShapeDtypeStruct((16, 128), jnp.float32),
            jax.ShapeDtypeStruct((1, 1), jnp.int32),
        ),
        in_specs=[vmem] * 4,
        out_specs=(vmem, vmem, pl.BlockSpec(memory_space=pltpu.SMEM)),
        interpret=interpret,
    )(pattern_p, pattern_sq, pattern_cube, placement.reshape(1, 64))


def split(x):
    hi = x.astype(jnp.bfloat16)
    lo = (x - hi.astype(jnp.float32)).astype(jnp.bfloat16)
    return hi, lo


def product(left, right):
    lh, ll = left
    rh, rl = split(right)
    lhs = jnp.concatenate([lh, lh, ll], axis=1)
    rhs = jnp.concatenate([rh, rl, rh], axis=0)
    return jnp.dot(lhs, rhs, preferred_element_type=jnp.float32)


class Ring:
    def __init__(self, part, size, me, plus, minus, ss, rs, base):
        up, down = lax.rem(me + 1, 4), lax.rem(me + 3, 4)
        cut = (size + 1) // 2
        own, left, right = part(me, 0, size), part(down, 0, size), part(up, 0, size)
        copy = lambda ref, n, dev: pltpu.make_async_remote_copy(
            src_ref=ref,
            dst_ref=ref,
            send_sem=ss.at[base + n],
            recv_sem=rs.at[base + n],
            device_id=dev,
            device_id_type=MESH,
        )
        self.copies = [
            copy(own, 0, plus),
            copy(own, 1, minus),
            copy(part(down, 0, cut), 2, plus),
            copy(part(up, cut, size - cut), 3, minus),
        ]

    def near(self):
        self.copies[0].start()
        self.copies[1].start()

    def far(self):
        self.copies[0].wait_recv()
        self.copies[2].start()
        self.copies[1].wait_recv()
        self.copies[3].start()

    def done(self):
        self.copies[2].wait_recv()
        self.copies[3].wait_recv()

    def sent(self):
        for c in self.copies:
            c.wait_send()


class Twin:
    def __init__(self, part, size, me, twin, ss, rs, base):
        self.copies = []
        for n in range(4):
            ref = part(lax.rem(me + n, 4), 0, size)
            self.copies.append(
                pltpu.make_async_remote_copy(
                    src_ref=ref,
                    dst_ref=ref,
                    send_sem=ss.at[base + n],
                    recv_sem=rs.at[base + n],
                    device_id=twin,
                    device_id_type=MESH,
                )
            )

    def start(self, *which):
        for n in which:
            self.copies[n].start()

    def recv(self, *which):
        for n in which:
            self.copies[n].wait_recv()

    def sent(self):
        for c in self.copies:
            c.wait_send()


COPIES = 16 + 16 + 4 * 8 + 5 * 8 + 1


def kernel(
    dens, ints, floats,
    out,
    a_buf, a_hi, a_lo, g0, g1, b0, b1, b2, b3, acc, ss, rs, own_sem,
):
    row, col = lax.axis_index("row"), lax.axis_index("col")
    z, y, x, core = row // 4, lax.rem(row, 4), col // 2, lax.rem(col, 2)
    up = lambda v: lax.rem(v + 1, 4)
    down = lambda v: lax.rem(v + 3, 4)
    yp, ym = (z * 4 + up(y), col), (z * 4 + down(y), col)
    zp, zm = (up(z) * 4 + y, col), (down(z) * 4 + y, col)
    xp, xm = (row, up(x) * 2 + core), (row, down(x) * 2 + core)
    twin = (row, x * 2 + 1 - core)
    pieces = (b0, b1, b2, b3)
    squares = ((g0, 0), (g1, 0), (a_buf, 0), (a_buf, 64))

    barrier = pltpu.get_barrier_semaphore()
    for dev in (yp, ym, zp, zm, xp, xm, twin):
        pl.semaphore_signal(barrier, inc=1, device_id=dev, device_id_type=MESH)

    def fetch(n, _):
        block = dens.at[
            pl.ds(pl.multiple_of(n // 8 * BLOCK, BLOCK), BLOCK),
            pl.ds(pl.multiple_of(lax.rem(n, 8) * BLOCK, BLOCK), BLOCK),
        ]
        pltpu.make_async_copy(block, b0.at[core * 32 + n], own_sem).start()
        return 0

    lax.fori_loop(0, 32, fetch, 0)
    zero = jnp.zeros((BLOCK, BLOCK), jnp.float32)
    for piece, at in zip(pieces, ZERO):
        piece[at] = zero
    a_buf[8 * PANEL] = zero

    base = 0
    half = PANEL // 2
    a_rings, a_twins = [], []
    for p in range(2):
        part = lambda m, lo, n, p=p: a_buf.at[pl.ds((m * 2 + core) * PANEL + p * half + lo, n)]
        a_rings.append(Ring(part, half, x, xp, xm, ss, rs, base))
        a_twins.append(Twin(part, half, x, twin, ss, rs, base + 4))
        base += 8
    g_rings, g_twins = [], []
    for ref, me, plus, minus in ((g0, y, yp, ym), (g1, z, zp, zm)):
        part = lambda m, lo, n, r=ref: r.at[pl.ds((m * 2 + core) * FIRST + lo, n)]
        g_rings.append(Ring(part, FIRST, me, plus, minus, ss, rs, base))
        g_twins.append(Twin(part, FIRST, me, twin, ss, rs, base + 4))
        base += 8
    b_rings = []
    for piece, cap in zip(pieces, CAPS):
        part0 = lambda m, lo, n, r=piece, c=cap: r.at[pl.ds(m * c + lo, n)]
        part1 = lambda m, lo, n, r=piece, c=cap: r.at[pl.ds((4 + m) * c + lo, n)]
        b_rings.append([
            Ring(part0, cap, z, zp, zm, ss, rs, base),
            Ring(part1, cap, y, yp, ym, ss, rs, base + 4),
        ])
        base += 8
    s_rings, s_twins = [], []
    for q, (ref, off) in enumerate(squares):
        s_rings.append([])
        s_twins.append([])
        parts = 2 if q == 3 else 1
        size = 8 // parts
        for p in range(parts):
            part = lambda m, lo, n, r=ref, o=off + p * size: r.at[pl.ds(o + (m * 2 + core) * 8 + lo, n)]
            s_rings[q].append(Ring(part, size, x, xp, xm, ss, rs, base))
            s_twins[q].append(Twin(part, size, x, twin, ss, rs, base + 4))
            base += 8
    raw = pltpu.make_async_remote_copy(
        src_ref=b0.at[pl.ds(core * 32, 32)],
        dst_ref=b0.at[pl.ds(core * 32, 32)],
        send_sem=ss.at[base],
        recv_sem=rs.at[base],
        device_id=twin,
        device_id_type=MESH,
    )

    near = lambda rings: [r.near() for r in rings]
    far = lambda rings: [r.far() for r in rings]
    done = lambda rings: [r.done() for r in rings]

    own = b0.at[pl.ds(core * 32, 32)]
    pltpu.make_async_copy(own, own, own_sem).wait()
    pl.semaphore_wait(barrier, 7)
    raw.start()
    raw.wait()

    def fill(s, _):
        g0[(y * 2 + core) * FIRST + s] = b0[ints[LISTS + 2, s]]
        g1[(z * 2 + core) * FIRST + s] = b0[ints[LISTS + 3, s]]
        return 0

    def panel(s, _):
        a_buf[col * PANEL + s] = b0[ints[LISTS + 4, s]]
        return 0

    lax.fori_loop(0, FIRST, fill, 0)
    lax.fori_loop(0, PANEL, panel, 0)
    near(g_rings)
    for t in g_twins:
        t.start(0)
    for p in range(2):
        a_rings[p].near()
        a_twins[p].start(0)
    far(g_rings)
    for t in g_twins:
        t.start(1, 3)
    done(g_rings)
    for t in g_twins:
        t.start(2)
    for t in g_twins:
        t.recv(0, 1, 2, 3)

    for q in range(4):

        def regroup(s, _, q=q):
            pieces[q][z * CAPS[q] + s] = g0[ints[LISTS, STARTS[q] + s]]
            pieces[q][(4 + y) * CAPS[q] + s] = g1[ints[LISTS + 1, STARTS[q] + s]]
            return 0

        lax.fori_loop(0, CAPS[q], regroup, 0)
        if q == 0:
            near(b_rings[q])
    for r in g_rings + g_twins:
        r.sent()

    def right_block(q, k, jj):
        block = pieces[q][ints[LOC + k, 8 + 2 * q + jj]]
        if q:
            block = block + pieces[q - 1][ints[LOC + k, 2 * q + jj]]
        return block

    def square(q, rows, lo, hi):
        tall = len(rows) * BLOCK

        def step(kk, _):
            k0 = kk * 4
            left = [
                jnp.concatenate([
                    jnp.concatenate([a[ints[LEFT + i, k0 + t]] for t in range(4)], axis=1)
                    for i in rows
                ], axis=0)
                for a in (a_hi, a_lo)
            ]
            right = jnp.concatenate([
                jnp.concatenate([right_block(q, k0 + t, jj) for jj in range(2)], axis=1)
                for t in range(4)
            ], axis=0)
            acc[0:tall, :] += product(left, right)
            return 0

        if lo == 0:
            acc[...] = jnp.zeros_like(acc)
        lax.fori_loop(lo, hi, step, 0, unroll=2 - (hi - lo) % 2)

    def send_square(q, rows, part):
        ref, off = squares[q]
        for n, i in enumerate(rows):
            for jj in range(2):
                ref[off + col * 8 + i * 2 + jj] = (
                    acc[n * BLOCK : (n + 1) * BLOCK, jj * BLOCK : (jj + 1) * BLOCK]
                    * floats[i, 2 * q + jj]
                )
        s_rings[q][part].near()
        s_twins[q][part].start(0)

    def cube(q, pairs, lo=0, hi=4):
        ref, off = squares[q]

        def step(o, _):
            o = o + jnp.where(o == 2, 1, 0) - jnp.where(o == 3, 1, 0)
            cd = lax.rem(x + o, 4) * 2
            left = split(jnp.concatenate([
                jnp.concatenate([ref[off + (cd + t // 2) * 8 + i * 2 + t % 2] for t in range(4)], axis=1)
                for i in range(4)
            ], axis=0))
            for n in pairs:
                right = jnp.concatenate([
                    jnp.concatenate([right_block(n, (cd + t // 2) * 8 + 2 * q + t % 2, jj) for jj in range(2)], axis=1)
                    for t in range(4)
                ], axis=0)
                out[:, n * 256 : (n + 1) * 256] += product(left, right)
            return 0

        lax.fori_loop(lo, hi, step, 0, unroll=2 - (hi - lo) % 2)

    def s_far(q, part=0):
        s_rings[q][part].far()
        s_twins[q][part].start(1, 3)

    def s_done(q):
        for r, t in zip(s_rings[q], s_twins[q]):
            r.done()
            t.start(2)

    def s_recv(q, *which):
        for t in s_twins[q]:
            t.recv(*which)

    every, top, bottom = range(4), range(2), range(2, 4)
    for p in range(2):
        a_rings[p].far()
        a_twins[p].start(1, 3)
    far(b_rings[0])
    near(b_rings[1])
    for p in range(2):
        a_rings[p].done()
        a_twins[p].start(2)
    for p in range(2):
        a_twins[p].recv(0, 1, 2, 3)

    def cut(n, _):
        a_hi[n], a_lo[n] = split(a_buf[n])
        return 0

    lax.fori_loop(0, 8 * PANEL + 1, cut, 0)
    for r in a_rings + a_twins:
        r.sent()
    out[...] = jnp.zeros_like(out)
    done(b_rings[0])
    square(0, every, 0, 16)
    send_square(0, every, 0)
    far(b_rings[1])
    near(b_rings[2])
    done(b_rings[1])
    square(1, every, 0, 8)
    s_far(0)
    square(1, every, 8, 16)
    send_square(1, every, 0)
    far(b_rings[2])
    near(b_rings[3])
    s_done(0)
    s_recv(0, 0, 1, 2, 3)
    cube(0, (0, 1))
    done(b_rings[2])
    square(2, every, 0, 8)
    s_far(1)
    square(2, every, 8, 16)
    send_square(2, every, 0)
    cube(0, (2,))
    far(b_rings[3])
    s_done(1)
    s_recv(1, 0, 1, 2, 3)
    cube(1, (0, 1, 2))
    done(b_rings[3])
    square(3, top, 0, 8)
    s_far(2)
    square(3, top, 8, 16)
    send_square(3, top, 0)
    square(3, bottom, 0, 16)
    send_square(3, bottom, 1)
    cube(0, (3,))
    s_done(2)
    s_far(3, 0)
    cube(1, (3,))
    s_recv(2, 0, 1, 3)
    cube(2, (0, 1, 2, 3), 0, 3)
    s_far(3, 1)
    s_recv(2, 2)
    cube(2, (0, 1, 2, 3), 3, 4)
    s_recv(3, 0)
    cube(3, (0, 1, 2, 3), 0, 1)
    s_done(3)
    s_recv(3, 1, 3)
    cube(3, (0, 1, 2, 3), 1, 3)
    s_recv(3, 2)
    cube(3, (0, 1, 2, 3), 3, 4)
    for i in range(4):
        for q in range(4):
            for jj in range(2):
                j = 2 * q + jj
                at = (slice(i * BLOCK, (i + 1) * BLOCK), slice(j * BLOCK, (j + 1) * BLOCK))
                out[at] = 3.0 * squares[q][0][squares[q][1] + col * 8 + i * 2 + jj] - 2.0 * (out[at] * floats[8 + i, j])

    for pair in b_rings:
        for r in pair:
            r.sent()
    for parts in s_rings + s_twins:
        for r in parts:
            r.sent()


def packed(density, ints, floats):
    smem = pl.BlockSpec(memory_space=pltpu.SMEM)
    vmem = pl.BlockSpec(memory_space=pltpu.VMEM)
    blocks = lambda n: pltpu.VMEM((n, BLOCK, BLOCK), jnp.float32)
    return pl.pallas_call(
        kernel,
        out_shape=jax.ShapeDtypeStruct(density.shape, jnp.float32),
        in_specs=[pl.BlockSpec(memory_space=pl.ANY), smem, smem],
        out_specs=vmem,
        scratch_shapes=[
            blocks(8 * PANEL + 1),
            pltpu.VMEM((8 * PANEL + 1, BLOCK, BLOCK), jnp.bfloat16),
            pltpu.VMEM((8 * PANEL + 1, BLOCK, BLOCK), jnp.bfloat16),
            blocks(8 * FIRST),
            blocks(8 * FIRST),
            *[blocks(at + 1) for at in ZERO],
            pltpu.VMEM((512, 256), jnp.float32),
            pltpu.SemaphoreType.DMA((COPIES,)),
            pltpu.SemaphoreType.DMA((COPIES,)),
            pltpu.SemaphoreType.DMA,
        ],
        compiler_params=pltpu.CompilerParams(
            collective_id=0, has_side_effects=True, vmem_limit_bytes=127 * 2**19
        ),
        cost_estimate=pl.CostEstimate(flops=6 * 2**34, bytes_accessed=2**22, transcendentals=0),
    )(density, ints, floats)


def body(density, pattern_p, pattern_sq, pattern_cube, placement):
    ints, floats, fits = make_plan(pattern_p, pattern_sq, pattern_cube, placement)
    return lax.cond(
        fits[0, 0] > 0,
        lambda: packed(density, ints, floats),
        lambda: dense(density, pattern_p, pattern_sq, pattern_cube, placement),
    )


def solution(mesh):
    return jax.shard_map(
        body,
        mesh=mesh,
        in_specs=(P("row", "col"), P(), P(), P(), P()),
        out_specs=P("row", "col"),
        check_vma=False,
    )
```
